32 devices in a mesh: rep: 2 (over y), ep: 4 (over z), tr: 2 (over x), tc: 2 (over core).
Axes of the slice: x: 2, y: 2, z: 4, core: 2. Of those that a mesh axis runs over, the one named last changes fastest.
Arguments:
- residual: bfloat16 [2048, 6144], P(('rep', 'ep', 'tc'), 'tr'), parts along dimension 0, may hold values from -24 to 24
- query_rows: bfloat16 [2048, 6144], P(('rep', 'ep', 'tc'), 'tr'), parts along dimension 0, may hold values from -4.5 to 4.5
- key_rows: bfloat16 [2048, 1024], P(('rep', 'ep', 'tc'), 'tr'), parts along dimension 0, may hold values from -10 to 10
- value_rows: bfloat16 [2048, 1024], P(('rep', 'ep', 'tc'), 'tr'), parts along dimension 0, may hold values from -6 to 6
- segments: int32 [2048], P('rep'), parts along dimension 0, may hold values from 0 to 7, never falling along the last dimension, each value on 1 to 512 neighbouring positions
- routes: int32 [2048, 2], P(('rep', 'ep', 'tc')), parts along dimension 0, may hold values from 0 to 7, as said below
- gate_weights: float32 [2048, 2], P(('rep', 'ep', 'tc')), parts along dimension 0, may hold values from 0.3 to 1
- norm_gain: float32 [6144], P('tr'), may hold values from 0.1 to 1.9
- w_gate: bfloat16 [6144, 16384], P('tr', ('ep', 'tc')), may hold values from -0.078125 to 0.078125
- w_up: bfloat16 [6144, 16384], P('tr', ('ep', 'tc')), may hold values from -0.078125 to 0.078125
- w_down: bfloat16 [16384, 6144], P(('ep', 'tc'), 'tr'), may hold values from -0.0625 to 0.0625
Outputs:
- attention: bfloat16 [2048, 6144], P(('rep', 'ep', 'tc'), 'tr'), parts along dimension 0
- expert_mix: bfloat16 [2048, 6144], P(('rep', 'ep', 'tc'), 'tr'), parts along dimension 0
The draws below stay inside these ranges and needn't reach their ends.
There are 2 independent parts, one for each index of `rep`. The reference program is written for one: setup_inputs(seed, part) draws one part's arguments, and reference() takes and returns one part's arrays. A program takes and returns all parts, laid end to end along the dimension named above; an argument that names none is the same for every part. Nothing has to cross between parts.
Inputs may be any that keep to these rules, and one draw needn't show every extreme that they name: `routes`: each row names two different experts. The rows of one device (an aligned block of 128 rows) name each expert below 2 at most 32 times, and in every draw one expert below 2 is named exactly 32 times by the rows of every device.
All inputs are finite; a program needn't handle non-finite values.
Results may differ from the reference program's by a relative error of at most 0.024.
Values may be sent and summed in bfloat16 or wider, within the bound.
A program may use at most 128 MiB of HBM per device.

```python
import math
import jax
import jax.numpy as jnp
import numpy as np
from jax import lax

D = 6144
QH = 48
KVH = 8
HD = 128
EXPERTS = 8
TOPK = 2
EXPW = 2
FFW = 8192
TOK_DEV = 128
SEGS = 8
SEQ = 1024
N_EP = 4
N_TR = 2
N_TC = 2


def shared_keys(key):
    base_key = jax.random.fold_in(key, 0)
    base_keys = jnp.clip(jax.random.normal(base_key, (SEQ, KVH * HD), jnp.float32), -4.0, 4.0) * 2.5
    return base_keys


def draw_key_rows(key, part):
    base_keys = shared_keys(key)
    return base_keys.astype(jnp.bfloat16)


def draw_query_rows(key, part):
    key = jax.random.fold_in(key, 5)
    noise_rows = jnp.clip(jax.random.normal(key, (SEQ, QH * HD), jnp.float32), -4.5, 4.5)
    return noise_rows.astype(jnp.bfloat16)


def draw_residual(key, part):
    key = jax.random.fold_in(key, 3)
    value_key, scale_key = jax.random.split(key)
    column_frac = jnp.arange(D, dtype=jnp.float32) / D
    values = jnp.clip(jax.random.normal(value_key, (SEQ, D), jnp.float32), -4.5, 4.5)
    row_scale = jnp.exp(jax.random.uniform(scale_key, (SEQ, 1), jnp.float32, math.log(0.3), math.log(3.0)))
    col_scale = jnp.sqrt(1.0 + 2.0 * column_frac)
    return (values * row_scale * col_scale[None, :]).astype(jnp.bfloat16)


def rank_of(key, block_count):
    token_index = jnp.arange(TOK_DEV, dtype=jnp.int32)
    scores = jax.random.randint(key, (block_count, TOK_DEV), 0, 1 << 16) * TOK_DEV + token_index[None, :]
    order = jnp.argsort(scores, axis=1)
    return jnp.argsort(order, axis=1)


def draw_routes(key, part):
    key = jax.random.fold_in(key, 11)
    block_count = SEQ // TOK_DEV
    capacity = TOK_DEV // 4
    subkeys = jax.random.split(key, 7)
    hot_expert = jax.random.randint(subkeys[0], (), 0, EXPW)
    cold_expert = (hot_expert + 1) % EXPW
    named_hot = rank_of(subkeys[1], block_count) < capacity
    counts = jax.random.randint(subkeys[2], (block_count, 1), capacity // 4, capacity // 2 + 1)
    named_cold = rank_of(subkeys[3], block_count) < counts
    spare_count = EXPERTS - EXPW
    first_pick = EXPW + jax.random.randint(subkeys[4], (block_count, TOK_DEV), 0, spare_count)
    second_pick = EXPW + (first_pick - EXPW + 1 + jax.random.randint(subkeys[5], (block_count, TOK_DEV), 0, spare_count - 1)) % spare_count
    leading = jnp.where(named_hot, hot_expert, jnp.where(named_cold, cold_expert, first_pick))
    trailing = jnp.where(named_hot & named_cold, cold_expert, jnp.where(named_hot | named_cold, first_pick, second_pick))
    swapped = jax.random.randint(subkeys[6], (block_count, TOK_DEV), 0, 2) == 1
    left_pick = jnp.where(swapped, trailing, leading)
    right_pick = jnp.where(swapped, leading, trailing)
    return jnp.stack([left_pick, right_pick], axis=-1).reshape(SEQ, 2).astype(jnp.int32)


def steps_of(own_key, extent, shards, smallest, largest):
    gain, own = 1.0, jax.random.fold_in(own_key, 6)
    for dim, blocks in shards:
        steps = jnp.exp(jax.random.uniform(jax.random.fold_in(own, dim), (blocks,), jnp.float32, smallest / len(shards), largest / len(shards)))
        gain = gain * jnp.repeat(steps, extent[dim] // blocks).reshape([-1 if axis == dim else 1 for axis in range(len(extent))])
    return gain


def profile(number_of, total, limit, lean):
    loads = [(1 << 20) // math.isqrt(grade ** lean) + 1 for grade in range(2, number_of + 1)]
    surplus, given = total - limit - (number_of - 1), [1] * (number_of - 1)
    while surplus > 0:
        movable = [i for i in range(number_of - 1) if given[i] < limit]
        pool, remaining = sum([loads[i] for i in movable]), surplus
        for i in movable:
            extra = min(limit - given[i], max(1, remaining * loads[i] // pool), surplus)
            given[i] = given[i] + extra
            surplus = surplus - extra
    return np.array([limit] + given)


def ragged_sizes(own_key, amount, total, reach, lean):
    if amount == 2:
        one = jax.random.randint(own_key, (), max(1, total - reach), min(reach, total - 1) + 1)
        return jnp.stack([one, total - one])
    sizes = jnp.asarray(profile(amount, total, reach, lean), jnp.int32)
    pairs = (amount - 1) // 2
    donor, sink = sizes[1:1 + 2 * pairs:2], sizes[2:2 + 2 * pairs:2]
    room = jnp.minimum(donor - 1, reach - sink)
    passed = jax.random.randint(jax.random.fold_in(own_key, 1), (pairs,), 0, 1 << 20) % (room + 1)
    sizes = sizes.at[1:1 + 2 * pairs:2].set(donor - passed).at[2:2 + 2 * pairs:2].set(sink + passed)
    return sizes[jax.random.permutation(jax.random.fold_in(own_key, 2), amount)]


def noise(rng, shape, deviation, bound, pieces=(), held_as=jnp.bfloat16):
    array = jax.random.normal(rng, shape, jnp.float32) * deviation
    if len(pieces) > 0:
        array = steps_of(rng, shape, pieces, -0.22, 0.18) * array
    return jnp.clip(array, min=-bound, max=bound).astype(held_as)


def setup_inputs(seed: int = 0, part: int = 0) -> dict:
    key_of = jax.random.split(jax.random.key(seed), 12)
    part_splits = jax.random.split(jax.random.fold_in(key_of[11], part), 12)
    return {
        "residual": draw_residual(jax.random.fold_in(jax.random.fold_in(key_of[11], part), 71), part),
        "query_rows": draw_query_rows(jax.random.fold_in(jax.random.fold_in(key_of[11], part), 71), part),
        "key_rows": draw_key_rows(jax.random.fold_in(jax.random.fold_in(key_of[11], part), 71), part),
        "value_rows": noise(part_splits[3], (SEQ, KVH * HD), 1.0, 6.0, ((0, 8), (1, 2))),
        "segments": jnp.searchsorted(jnp.cumsum(ragged_sizes(part_splits[4], SEGS, SEQ, SEQ // 2, 1)), jnp.arange(SEQ), side="right").astype(jnp.int32),
        "routes": draw_routes(jax.random.fold_in(jax.random.fold_in(key_of[11], part), 71), part),
        "gate_weights": jnp.clip(0.3 + 0.7 * jax.random.uniform(part_splits[6], (SEQ, TOPK), jnp.float32) ** steps_of(part_splits[6], (SEQ, TOPK), ((0, 8),), -0.2, 0.2), 0.3, 1.0),
        "norm_gain": jnp.clip(1.0 + 0.18 * jax.random.normal(key_of[7], (D,), jnp.float32), 0.1, 1.9),
        "w_gate": noise(key_of[8], (D, EXPW * FFW), D ** -0.5, 0.078125, ((0, 2), (1, 8))),
        "w_up": noise(key_of[9], (D, EXPW * FFW), D ** -0.5, 0.078125, ((0, 2), (1, 8))),
        "w_down": noise(key_of[10], (EXPW * FFW, D), FFW ** -0.5, 0.0625, ((0, 8), (1, 2))),
    }


masked_score = -1e+30

def settle(values):
    return lax.optimization_barrier(values.astype(jnp.bfloat16)).astype(jnp.float32)

def attend_head(query_head, key_head, value_head, visible):
    scores = jnp.einsum('gsd,td->gst', query_head.astype(jnp.float32), key_head.astype(jnp.float32), precision=lax.Precision.HIGHEST) / math.sqrt(HD)
    scores = jnp.where(visible[None], scores, masked_score)
    highest = lax.optimization_barrier(jnp.max(scores, axis=2, keepdims=True))
    exponent = jnp.where(visible[None], jnp.exp(scores - highest), 0.0)
    denominator = lax.optimization_barrier(jnp.sum(exponent, axis=2, keepdims=True))
    rounded = settle(exponent)
    weighted = jnp.einsum('gst,td->gsd', rounded, value_head.astype(jnp.float32), precision=lax.Precision.HIGHEST)
    return weighted / denominator

def reference(residual, query_rows, key_rows, value_rows, segments, routes, gate_weights, norm_gain, w_gate, w_up, w_down):
    length = residual.shape[0]
    group_size = QH // KVH
    position = jnp.arange(length, dtype=jnp.int32)
    visible = (position[None, :] <= position[:, None]) & (segments[None, :] == segments[:, None])
    query_heads = query_rows.reshape(length, KVH, group_size, HD).transpose(1, 2, 0, 3)
    key_heads = key_rows.reshape(length, KVH, HD).transpose(1, 0, 2)
    value_heads = value_rows.reshape(length, KVH, HD).transpose(1, 0, 2)
    outcome = lax.map(lambda operands: attend_head(operands[0], operands[1], operands[2], visible), (query_heads, key_heads, value_heads))
    attention = outcome.transpose(2, 0, 1, 3).reshape(length, D).astype(jnp.bfloat16)
    mixed_rows = (residual.astype(jnp.float32) + attention.astype(jnp.float32)).astype(jnp.bfloat16)
    mixed_wide = mixed_rows.astype(jnp.float32)
    inv_rms = lax.rsqrt(lax.optimization_barrier(jnp.mean(mixed_wide * mixed_wide, axis=1, keepdims=True)) + 1e-05)
    normed = (mixed_wide * inv_rms * norm_gain[None, :]).astype(jnp.bfloat16)
    expert_mix = jnp.zeros((length, D), jnp.float32)
    feature_block = D // N_TR
    piece_count = N_EP * N_TC // EXPW
    hidden_block = FFW // piece_count
    most_rows = length // 4
    for expert in range(EXPW):
        matches = routes == expert
        chosen_mask = jnp.any(matches, axis=1)
        weight_col = lax.optimization_barrier(jnp.sum(jnp.where(matches, gate_weights, 0.0), axis=1))
        chosen = jnp.nonzero(chosen_mask, size=most_rows, fill_value=0)[0].astype(jnp.int32)
        live_rows = jnp.arange(most_rows, dtype=jnp.int32) < jnp.sum(chosen_mask.astype(jnp.int32))
        picked = normed[chosen]
        low_col = expert * FFW
        gate_sum = jnp.zeros((most_rows, FFW), jnp.float32)
        up_sum = jnp.zeros((most_rows, FFW), jnp.float32)
        for block_index in range(N_TR):
            start_feat = block_index * feature_block
            inputs = picked[:, start_feat:start_feat + feature_block]
            gate_sum = gate_sum + settle(jnp.dot(inputs, w_gate[start_feat:start_feat + feature_block, low_col:low_col + FFW], preferred_element_type=jnp.float32))
            up_sum = up_sum + settle(jnp.dot(inputs, w_up[start_feat:start_feat + feature_block, low_col:low_col + FFW], preferred_element_type=jnp.float32))
        hidden = (jax.nn.silu(gate_sum) * up_sum).astype(jnp.bfloat16)
        result = jnp.zeros((most_rows, D), jnp.float32)
        for piece_index in range(piece_count):
            start_hidden = piece_index * hidden_block
            result = result + settle(jnp.dot(hidden[:, start_hidden:start_hidden + hidden_block], w_down[low_col + start_hidden:low_col + start_hidden + hidden_block, :], preferred_element_type=jnp.float32))
        contribution = jnp.where(live_rows[:, None], weight_col[chosen][:, None] * result, 0.0)
        expert_mix = expert_mix.at[chosen].add(contribution)
    return (attention, expert_mix.astype(jnp.bfloat16))
```

```python
import math

import jax
import jax.numpy as jnp
from jax import lax
from jax.experimental import pallas as pl
from jax.experimental.pallas import tpu as pltpu
from jax.sharding import PartitionSpec as P

D = 6144
QH = 48
KVH = 8
HD = 128
EXPW = 2


masked_score = -1e30
key_block = 512


def score_block(
    running, key_piece, value_piece, offset, query_heads, row_pos, row_seg, segments, score_scale
):
    best_score, denominator, accumulated = running
    length = key_piece.shape[0]
    head_count = query_heads.shape[0]
    key_heads = key_piece.reshape(length, head_count, HD)
    value_heads = value_piece.reshape(length, head_count, HD)
    key_pos = offset + jnp.arange(length, dtype=jnp.int32)
    key_seg = lax.dynamic_slice_in_dim(segments, offset, length)
    visible = (key_pos[None, :] <= row_pos[:, None]) & (key_seg[None, :] == row_seg[:, None])
    scores = (
        jnp.einsum("hrd,khd->hrk", query_heads, key_heads, preferred_element_type=jnp.float32)
        * score_scale
    )
    scores = jnp.where(visible[None], scores, masked_score)
    new_best = jnp.maximum(best_score, jnp.max(scores, axis=2))
    exponent = jnp.where(visible[None], jnp.exp(scores - new_best[:, :, None]), 0.0)
    factor = jnp.exp(best_score - new_best)
    denominator = denominator * factor + jnp.sum(exponent, axis=2)
    accumulated = accumulated * factor[:, :, None] + jnp.einsum(
        "hrk,khd->hrd",
        exponent.astype(jnp.bfloat16),
        value_heads,
        preferred_element_type=jnp.float32,
    )
    return (new_best, denominator, accumulated)


def fold_context(running, pieces, start, query_heads, row_pos, row_seg, segments, score_scale):
    key_piece, value_piece = pieces
    total_rows = key_piece.shape[0]
    for offset_rows in range(0, total_rows, key_block):
        width_rows = min(key_block, total_rows - offset_rows)
        running = score_block(
            running,
            key_piece[offset_rows : offset_rows + width_rows],
            value_piece[offset_rows : offset_rows + width_rows],
            start + offset_rows,
            query_heads,
            row_pos,
            row_seg,
            segments,
            score_scale,
        )
    return running


def shards(
    residual,
    query_rows,
    key_rows,
    value_rows,
    segments,
    routes,
    gate_weights,
    norm_gain,
    w_gate,
    w_up,
    w_down,
):
    tokens = residual.shape[0]
    feature_width = residual.shape[1]
    kv_count = key_rows.shape[1] // HD
    group_size = QH // KVH
    row_count = tokens * group_size
    first_token = lax.axis_index(("ep", "tc")) * tokens
    token_pos = first_token + jnp.arange(tokens, dtype=jnp.int32)
    token_seg = lax.dynamic_slice_in_dim(segments, first_token, tokens)
    row_pos = jnp.repeat(token_pos, group_size)
    row_seg = jnp.repeat(token_seg, group_size)
    query_heads = (
        query_rows.reshape(tokens, kv_count, group_size, HD)
        .transpose(1, 0, 2, 3)
        .reshape(kv_count, row_count, HD)
    )
    score_scale = 1.0 / math.sqrt(HD)
    initial = (
        jnp.full((kv_count, row_count), masked_score, jnp.float32),
        jnp.zeros((kv_count, row_count), jnp.float32),
        jnp.zeros((kv_count, row_count, HD), jnp.float32),
    )
    folded = fold_context(
        initial,
        (
            lax.all_gather(key_rows, ("ep", "tc"), axis=0, tiled=True),
            lax.all_gather(value_rows, ("ep", "tc"), axis=0, tiled=True),
        ),
        jnp.int32(0),
        query_heads,
        row_pos,
        row_seg,
        segments,
        score_scale,
    )
    heads_out = folded[2] / folded[1][:, :, None]
    attention = (
        heads_out.reshape(kv_count, tokens, group_size, HD)
        .transpose(1, 0, 2, 3)
        .reshape(tokens, feature_width)
        .astype(jnp.bfloat16)
    )
    mixed_rows = (residual.astype(jnp.float32) + attention.astype(jnp.float32)).astype(jnp.bfloat16)
    mixed_wide = mixed_rows.astype(jnp.float32)
    squares = lax.psum(jnp.sum(mixed_wide * mixed_wide, axis=1), "tr")
    inv_rms = lax.rsqrt(squares / D + 1e-05)
    normed = (mixed_wide * inv_rms[:, None] * norm_gain[None, :]).astype(jnp.bfloat16)
    capacity = tokens // 4
    expert_ids = jnp.arange(EXPW, dtype=jnp.int32)
    matches = routes[:, None, :] == expert_ids[None, :, None]
    chosen = jnp.any(matches, axis=2)
    weight_cols = jnp.sum(jnp.where(matches, gate_weights[:, None, :], 0.0), axis=2)
    slot_index = jnp.cumsum(chosen.astype(jnp.int32), axis=0) - 1
    slot_ids = jnp.arange(capacity, dtype=jnp.int32)
    placement_table = (slot_index.T[:, None, :] == slot_ids[None, :, None]) & chosen.T[:, None, :]
    packed = jnp.einsum(
        "ect,td->ecd",
        placement_table.astype(jnp.bfloat16),
        normed,
        preferred_element_type=jnp.float32,
    ).astype(jnp.bfloat16)
    ep_count = lax.axis_size("ep")
    tc_count = lax.axis_size("tc")
    share_count = ep_count // EXPW
    spread = jnp.repeat(packed, share_count, axis=0)
    outgoing = jnp.broadcast_to(
        spread[:, None], (ep_count, tc_count, capacity, feature_width)
    ).reshape(ep_count * tc_count, capacity, feature_width)
    arrived = lax.all_to_all(outgoing, ("ep", "tc"), split_axis=0, concat_axis=0, tiled=True)
    slot_rows = arrived.reshape(ep_count * tc_count * capacity, feature_width)
    part_gate = jnp.dot(slot_rows, w_gate, preferred_element_type=jnp.float32)
    part_up = jnp.dot(slot_rows, w_up, preferred_element_type=jnp.float32)
    gate_sum, up_sum = (
        lax.psum(part_gate.astype(jnp.bfloat16), "tr").astype(jnp.float32),
        lax.psum(part_up.astype(jnp.bfloat16), "tr").astype(jnp.float32),
    )
    hidden = (jax.nn.silu(gate_sum) * up_sum).astype(jnp.bfloat16)
    down_part = (
        jnp.dot(hidden, w_down, preferred_element_type=jnp.float32)
        .astype(jnp.bfloat16)
        .reshape(ep_count * tc_count, capacity, feature_width)
    )
    returned = lax.all_to_all(down_part, ("ep", "tc"), split_axis=0, concat_axis=0, tiled=True)
    per_expert = jnp.sum(
        returned.astype(jnp.float32).reshape(EXPW, share_count * tc_count, capacity, feature_width),
        axis=1,
    )
    combine_table = placement_table.astype(jnp.float32) * weight_cols.T[:, None, :]
    expert_mix = jnp.einsum(
        "ect,ecd->td", combine_table, per_expert, precision=lax.Precision.HIGHEST
    ).astype(jnp.bfloat16)
    return (attention, expert_mix)


col_tiles = 4
row_slots = 32
MESH = pl.DeviceIdType.MESH


def layer_kernel(
    query_ref,
    key_ref,
    value_ref,
    residual_ref,
    segment_ref,
    route_ref,
    weight_ref,
    gain_ref,
    gate_hbm,
    up_hbm,
    down_hbm,
    attention_ref,
    mix_ref,
    gate_w,
    up_w,
    down_w,
    context,
    best,
    total,
    accumulated,
    mixed,
    sum_out,
    sum_in,
    slot_rows,
    cross_rows,
    parts,
    parts_in,
    hidden,
    down,
    down_in,
    reduced,
    outer_in,
    returned,
    load_sem,
    ctx_send,
    ctx_recv,
    sum_send,
    sum_recv,
    row_send,
    row_recv,
    part_send,
    part_recv,
    hid_send,
    hid_recv,
    down_send,
    down_recv,
    outer_send,
    outer_recv,
    ret_send,
    ret_recv,
):
    tokens, width = query_ref.shape
    kv_width = key_ref.shape[1]
    kv_count = kv_width // HD
    group = QH // KVH
    hidden_width = gate_w.shape[1]
    tile_h = hidden_width // col_tiles
    tile_f = width // col_tiles
    half = 2 * row_slots
    z = lax.axis_index("ep")
    x = lax.axis_index("tr")
    c = lax.axis_index("tc")
    pair = z // 2
    partner = z + 1 - 2 * lax.rem(z, 2)
    other_inner = 2 - pair
    other_outer = 3 - 3 * pair
    my_inner = 1 + pair
    my_outer = 3 * pair
    is_inner = z == my_inner
    sibling = {"tc": 1 - c}
    across = {"tr": 1 - x}

    loads = [
        pltpu.make_async_copy(gate_hbm, gate_w, load_sem.at[0]),
        pltpu.make_async_copy(up_hbm, up_w, load_sem.at[1]),
        pltpu.make_async_copy(down_hbm, down_w, load_sem.at[2]),
    ]
    for load in loads:
        load.start()

    barrier = pltpu.get_barrier_semaphore()
    for step in range(1, 4):
        there = lax.rem(z + step, 4)
        pl.semaphore_signal(barrier, inc=1, device_id={"ep": there}, device_id_type=MESH)
    pl.semaphore_signal(barrier, inc=1, device_id=sibling, device_id_type=MESH)
    pl.semaphore_signal(barrier, inc=1, device_id=across, device_id_type=MESH)

    def send(src, dst, send_sem, recv_sem, target):
        return pltpu.make_async_remote_copy(
            src_ref=src,
            dst_ref=dst,
            send_sem=send_sem,
            recv_sem=recv_sem,
            device_id=target,
            device_id_type=MESH,
        )

    own_ctx = pl.ds(pl.multiple_of(c * tokens, tokens), tokens)
    sib_ctx = pl.ds(pl.multiple_of((1 - c) * tokens, tokens), tokens)
    context[0, own_ctx, :kv_width] = key_ref[...]
    context[0, own_ctx, kv_width:] = value_ref[...]
    pl.semaphore_wait(barrier, 5)

    def ctx_copy(from_slot, to_slot, number, recv, target):
        return send(
            context.at[from_slot, own_ctx],
            context.at[to_slot, own_ctx],
            ctx_send.at[number],
            ctx_recv.at[recv],
            target,
        )

    up_chip = {"ep": lax.rem(z + 1, 4)}
    own_up = ctx_copy(0, 1, 0, 0, up_chip)
    near_up = ctx_copy(1, 2, 1, 1, up_chip)
    own_sib = ctx_copy(0, 0, 2, 2, sibling)
    near_sib = ctx_copy(1, 1, 3, 3, sibling)
    far_sib = ctx_copy(2, 2, 4, 4, sibling)

    @pl.when(z < 3)
    def _():
        own_up.start()

    own_sib.start()

    lane = lax.broadcasted_iota(jnp.int32, (tokens, tokens), 1)
    sub = lax.broadcasted_iota(jnp.int32, (tokens, tokens), 0)
    upto = jnp.where(sub <= lane, 1.0, 0.0).astype(jnp.bfloat16)

    def placement(expert):
        first = jnp.broadcast_to(route_ref[0:1, :], (tokens, tokens)) == expert
        second = jnp.broadcast_to(route_ref[1:2, :], (tokens, tokens)) == expert
        weight = jnp.where(
            first, jnp.broadcast_to(weight_ref[0:1, :], (tokens, tokens)), 0.0
        ) + jnp.where(second, jnp.broadcast_to(weight_ref[1:2, :], (tokens, tokens)), 0.0)
        named = jnp.where(first | second, 1.0, 0.0)
        order = jnp.dot(named.astype(jnp.bfloat16), upto, preferred_element_type=jnp.float32)
        wanted = (lax.rem(sub, row_slots) + 1).astype(jnp.float32)
        place = jnp.where((order == wanted) & (named > 0.5), 1.0, 0.0)
        return place, weight

    own_place, own_weight = placement(pair)
    cross_place, cross_weight = placement(1 - pair)

    scale = 1.0 / math.sqrt(HD)
    block = 2 * z + c
    row_seg = jnp.transpose(
        jnp.broadcast_to(segment_ref[pl.ds(block, 1), :].astype(jnp.float32), (tokens, tokens))
    )
    row_seg = jnp.concatenate([row_seg, row_seg], axis=1)

    def attend(slot):
        low = 2 * (z - slot)
        key_seg = jnp.concatenate(
            [segment_ref[pl.ds(low, 1), :], segment_ref[pl.ds(low + 1, 1), :]], axis=1
        ).astype(jnp.float32)
        visible = row_seg == jnp.broadcast_to(key_seg, (tokens, 2 * tokens))
        if slot == 0:
            key_pos = lax.broadcasted_iota(jnp.int32, (tokens, 2 * tokens), 1)
            row_pos = c * tokens + lax.broadcasted_iota(jnp.int32, (tokens, 2 * tokens), 0)
            visible = visible & (key_pos <= row_pos)
        bias = jnp.where(visible, 0.0, masked_score)

        def one_head(j, carry):
            heads = [
                query_ref[:, pl.ds(pl.multiple_of((j * group + g) * HD, HD), HD)]
                for g in range(group)
            ]
            queries = jnp.concatenate(heads, axis=0)
            keys = context[slot, :, pl.ds(pl.multiple_of(j * HD, HD), HD)]
            values = context[slot, :, pl.ds(pl.multiple_of(kv_width + j * HD, HD), HD)]
            scores = lax.dot_general(
                queries, keys, (((1,), (1,)), ((), ())), preferred_element_type=jnp.float32
            )
            scores = (scores * scale).reshape(group, tokens, 2 * tokens)
            scores = jnp.where((bias < -1.0)[None], masked_score, scores)
            scores = scores.reshape(group * tokens, 2 * tokens)
            peak = jnp.max(scores, axis=1, keepdims=True)
            if slot > 0:
                old = best[j][:, :1]
                peak = jnp.maximum(peak, old)
            exponent = jnp.exp(scores - peak)
            amount = jnp.sum(exponent, axis=1, keepdims=True)
            product = jnp.dot(
                exponent.astype(jnp.bfloat16), values, preferred_element_type=jnp.float32
            )
            if slot > 0:
                factor = jnp.exp(old - peak)
                amount = amount + total[j][:, :1] * factor
                product = product + accumulated[j] * factor
            best[j] = jnp.broadcast_to(peak, (group * tokens, HD))
            total[j] = jnp.broadcast_to(amount, (group * tokens, HD))
            accumulated[j] = product
            return carry

        lax.fori_loop(0, kv_count, one_head, 0)

    own_sib.wait_recv()
    attend(0)

    @pl.when(z >= 1)
    def _():
        own_up.wait_recv()

        @pl.when(z < 3)
        def _():
            near_up.start()

        near_sib.start()
        near_sib.wait_recv()
        attend(1)

    @pl.when(z >= 2)
    def _():
        near_up.wait_recv()
        far_sib.start()
        far_sib.wait_recv()
        attend(2)

    squares = jnp.zeros((tokens, HD), jnp.float32)

    def finish_head(j, squares):
        for g in range(group):
            rows = slice(g * tokens, (g + 1) * tokens)
            cols = pl.ds(pl.multiple_of((j * group + g) * HD, HD), HD)
            result = (accumulated[j, rows, :] / total[j, rows, :]).astype(jnp.bfloat16)
            attention_ref[:, cols] = result
            both = (
                residual_ref[:, cols].astype(jnp.float32) + result.astype(jnp.float32)
            ).astype(jnp.bfloat16)
            mixed[:, cols] = both
            wide = both.astype(jnp.float32)
            squares = squares + wide * wide
        return squares

    squares = lax.fori_loop(0, kv_count, finish_head, squares)
    my_sum = jnp.broadcast_to(jnp.sum(jnp.transpose(squares), axis=0, keepdims=True), (8, tokens))
    sum_out[...] = my_sum
    sum_copy = send(sum_out, sum_in, sum_send, sum_recv, across)
    sum_copy.start()
    sum_copy.wait_recv()
    both_sums = jnp.broadcast_to((my_sum + sum_in[...])[0:1, :], (tokens, tokens))
    inv_rms = jnp.transpose(lax.rsqrt(both_sums / D + 1e-05))[:, :1]
    picks = jnp.concatenate([own_place[:row_slots], cross_place[:row_slots]], axis=0).astype(
        jnp.bfloat16
    )
    own_near = pl.ds(pl.multiple_of(c * half, row_slots), row_slots)
    own_far = pl.ds(pl.multiple_of(c * half + row_slots, row_slots), row_slots)

    def pack(m, carry):
        cols = pl.ds(pl.multiple_of(m * tile_f, tile_f), tile_f)
        normed = (mixed[:, cols].astype(jnp.float32) * inv_rms * gain_ref[:, cols]).astype(
            jnp.bfloat16
        )
        packed = jnp.dot(picks, normed, preferred_element_type=jnp.float32).astype(jnp.bfloat16)
        slot_rows[0, own_near, cols] = packed[:row_slots]
        cross_rows[:, cols] = packed[row_slots:]
        return carry

    lax.fori_loop(0, col_tiles, pack, 0)

    def row_copy(chunk, place, number, recv, target):
        return send(
            slot_rows.at[chunk, place],
            slot_rows.at[chunk, place],
            row_send.at[number],
            row_recv.at[recv],
            target,
        )

    to_partner = send(
        slot_rows.at[0, own_near],
        slot_rows.at[0, own_far],
        row_send.at[0],
        row_recv.at[0],
        {"ep": partner},
    )
    cross_target = {"ep": other_inner}
    from_inner = send(
        cross_rows, slot_rows.at[1, own_near], row_send.at[1], row_recv.at[1], cross_target
    )
    from_outer = send(
        cross_rows, slot_rows.at[1, own_far], row_send.at[1], row_recv.at[2], cross_target
    )
    own_share = row_copy(0, own_near, 2, 3, sibling)
    partner_share = row_copy(0, own_far, 3, 4, sibling)
    inner_share = row_copy(1, own_near, 4, 5, sibling)
    outer_share = row_copy(1, own_far, 5, 6, sibling)
    pass_inner = row_copy(1, own_near, 6, 1, {"ep": my_outer})
    pass_outer = row_copy(1, own_far, 7, 2, {"ep": my_outer})

    to_partner.start()

    @pl.when(is_inner)
    def _():
        from_inner.start()

    @pl.when(jnp.logical_not(is_inner))
    def _():
        from_outer.start()

    own_share.start()

    def part_copy(chunk, n):
        number = chunk * col_tiles + n
        rows = pl.ds(pl.multiple_of((1 - x) * half, half), half)
        return send(
            parts.at[number, rows],
            parts_in.at[number],
            part_send.at[number],
            part_recv.at[number],
            across,
        )

    def hidden_copy(chunk, n):
        number = chunk * col_tiles + n
        rows = pl.ds(pl.multiple_of(x * half, half), half)
        return send(
            hidden.at[number, rows],
            hidden.at[number, rows],
            hid_send.at[number],
            hid_recv.at[number],
            across,
        )

    def gate_up(chunk):
        def one_tile(n, carry):
            cols = pl.ds(pl.multiple_of(n * tile_h, tile_h), tile_h)
            number = chunk * col_tiles + n
            parts[number, :, :tile_h] = jnp.dot(
                slot_rows[chunk], gate_w[:, cols], preferred_element_type=jnp.float32
            ).astype(jnp.bfloat16)
            parts[number, :, tile_h:] = jnp.dot(
                slot_rows[chunk], up_w[:, cols], preferred_element_type=jnp.float32
            ).astype(jnp.bfloat16)
            part_copy(chunk, n).start()
            return carry

        lax.fori_loop(0, col_tiles, one_tile, 0)

    def activate(chunk):
        def one_tile(n, carry):
            number = chunk * col_tiles + n
            part_copy(chunk, n).wait_recv()
            rows = pl.ds(pl.multiple_of(x * half, half), half)
            sums = parts[number, rows, :].astype(jnp.float32) + parts_in[number].astype(
                jnp.float32
            )
            gate = sums[:, :tile_h]
            hidden[number, rows, :] = (
                gate / (1.0 + jnp.exp(-gate)) * sums[:, tile_h:]
            ).astype(jnp.bfloat16)
            hidden_copy(chunk, n).start()
            return carry

        lax.fori_loop(0, col_tiles, one_tile, 0)

    def await_hidden(chunk):
        def one_tile(n, carry):
            hidden_copy(chunk, n).wait_recv()
            return carry

        lax.fori_loop(0, col_tiles, one_tile, 0)

    def down_copy(chunk, m):
        number = chunk * col_tiles + m
        rows = pl.ds(pl.multiple_of((1 - c) * half, half), half)
        return send(
            down.at[number, rows],
            down_in.at[number],
            down_send.at[number],
            down_recv.at[number],
            sibling,
        )

    def project(chunk):
        def one_tile(m, carry):
            cols = pl.ds(pl.multiple_of(m * tile_f, tile_f), tile_f)
            number = chunk * col_tiles + m
            units = jnp.concatenate(
                [hidden[chunk * col_tiles + n] for n in range(col_tiles)], axis=1
            )
            down[number] = jnp.dot(
                units, down_w[:, cols], preferred_element_type=jnp.float32
            ).astype(jnp.bfloat16)
            down_copy(chunk, m).start()
            return carry

        lax.fori_loop(0, col_tiles, one_tile, 0)

    def chip_sum(chunk, m):
        number = chunk * col_tiles + m
        down_copy(chunk, m).wait_recv()
        rows = pl.ds(pl.multiple_of(c * half, half), half)
        return down[number, rows, :].astype(jnp.float32) + down_in[number].astype(jnp.float32)

    near_rows = pl.ds(0, row_slots)
    far_rows = pl.ds(row_slots, row_slots)
    cross_back = pl.ds(half, row_slots)

    def partner_back(m):
        return send(
            reduced.at[m, far_rows],
            returned.at[m, far_rows],
            ret_send.at[m],
            ret_recv.at[m],
            {"ep": partner},
        )

    def outer_copy(m):
        return send(
            reduced.at[col_tiles + m],
            outer_in.at[m],
            outer_send.at[m],
            outer_recv.at[m],
            {"ep": my_inner},
        )

    def inner_back(m):
        return send(
            reduced.at[col_tiles + m, near_rows],
            returned.at[m, cross_back],
            ret_send.at[col_tiles + m],
            ret_recv.at[col_tiles + m],
            {"ep": other_inner},
        )

    def outer_back(m):
        return send(
            reduced.at[col_tiles + m, far_rows],
            returned.at[m, cross_back],
            ret_send.at[2 * col_tiles + m],
            ret_recv.at[col_tiles + m],
            {"ep": other_outer},
        )

    to_partner.wait_recv()
    partner_share.start()
    own_share.wait_recv()
    partner_share.wait_recv()
    loads[0].wait()
    loads[1].wait()
    gate_up(0)

    from_inner.wait_recv()
    inner_share.start()

    @pl.when(is_inner)
    def _():
        pass_inner.start()

    from_outer.wait_recv()
    outer_share.start()

    @pl.when(is_inner)
    def _():
        pass_outer.start()

    activate(0)
    inner_share.wait_recv()
    outer_share.wait_recv()
    gate_up(1)
    loads[2].wait()
    await_hidden(0)
    project(0)

    def return_own(m, carry):
        sums = chip_sum(0, m).astype(jnp.bfloat16)
        returned[m, near_rows, :] = sums[:row_slots]
        reduced[m] = sums
        partner_back(m).start()
        return carry

    lax.fori_loop(0, col_tiles, return_own, 0)

    activate(1)
    await_hidden(1)
    project(1)

    @pl.when(jnp.logical_not(is_inner))
    def _():
        def hand_over(m, carry):
            reduced[col_tiles + m] = chip_sum(1, m).astype(jnp.bfloat16)
            outer_copy(m).start()
            return carry

        lax.fori_loop(0, col_tiles, hand_over, 0)

    @pl.when(is_inner)
    def _():
        def hand_back(m, carry):
            sums = chip_sum(1, m)
            outer_copy(m).wait_recv()
            reduced[col_tiles + m] = (sums + outer_in[m].astype(jnp.float32)).astype(jnp.bfloat16)
            outer_back(m).start()
            inner_back(m).start()
            return carry

        lax.fori_loop(0, col_tiles, hand_back, 0)

    own_spread = jnp.transpose(own_place)[:, :half].astype(jnp.bfloat16)
    cross_spread = jnp.transpose(cross_place)[:, :row_slots].astype(jnp.bfloat16)
    own_scale = jnp.transpose(own_weight)[:, :1]
    cross_scale = jnp.transpose(cross_weight)[:, :1]

    def combine(m, carry):
        cols = pl.ds(pl.multiple_of(m * tile_f, tile_f), tile_f)
        partner_back(m).wait_recv()
        own_part = jnp.dot(own_spread, returned[m, :half, :], preferred_element_type=jnp.float32)
        inner_back(m).wait_recv()
        cross_part = jnp.dot(
            cross_spread, returned[m, half:, :], preferred_element_type=jnp.float32
        )
        mix_ref[:, cols] = (own_scale * own_part + cross_scale * cross_part).astype(jnp.bfloat16)
        return carry

    lax.fori_loop(0, col_tiles, combine, 0)

    @pl.when(z < 3)
    def _():
        own_up.wait_send()

    @pl.when((z >= 1) & (z < 3))
    def _():
        near_up.wait_send()

    own_sib.wait_send()

    @pl.when(z >= 1)
    def _():
        near_sib.wait_send()

    @pl.when(z >= 2)
    def _():
        far_sib.wait_send()

    sum_copy.wait_send()
    for copy in (to_partner, from_inner, own_share, partner_share, inner_share, outer_share):
        copy.wait_send()

    @pl.when(is_inner)
    def _():
        pass_inner.wait_send()
        pass_outer.wait_send()

    def drain(n, carry):
        for chunk in range(2):
            part_copy(chunk, n).wait_send()
            hidden_copy(chunk, n).wait_send()
            down_copy(chunk, n).wait_send()
        partner_back(n).wait_send()
        return carry

    lax.fori_loop(0, col_tiles, drain, 0)

    @pl.when(is_inner)
    def _():
        def drain_inner(m, carry):
            inner_back(m).wait_send()
            outer_back(m).wait_send()
            return carry

        lax.fori_loop(0, col_tiles, drain_inner, 0)

    @pl.when(jnp.logical_not(is_inner))
    def _():
        def drain_outer(m, carry):
            outer_copy(m).wait_send()
            return carry

        lax.fori_loop(0, col_tiles, drain_outer, 0)


def fused_shards(
    residual,
    query_rows,
    key_rows,
    value_rows,
    segments,
    routes,
    gate_weights,
    norm_gain,
    w_gate,
    w_up,
    w_down,
):
    tokens, width = residual.shape
    kv_width = key_rows.shape[1]
    kv_count = kv_width // HD
    group_rows = tokens * (QH // KVH)
    hidden_width = w_gate.shape[1]
    tile_h = hidden_width // col_tiles
    tile_f = width // col_tiles
    half = 2 * row_slots
    low = jnp.bfloat16
    vmem = pl.BlockSpec(memory_space=pltpu.VMEM)
    hbm = pl.BlockSpec(memory_space=pl.ANY)
    dma = pltpu.SemaphoreType.DMA
    return pl.pallas_call(
        layer_kernel,
        out_shape=(
            jax.ShapeDtypeStruct((tokens, width), low),
            jax.ShapeDtypeStruct((tokens, width), low),
        ),
        in_specs=[vmem] * 8 + [hbm] * 3,
        out_specs=(vmem, vmem),
        scratch_shapes=[
            pltpu.VMEM(w_gate.shape, low),
            pltpu.VMEM(w_up.shape, low),
            pltpu.VMEM(w_down.shape, low),
            pltpu.VMEM((3, 2 * tokens, 2 * kv_width), low),
            pltpu.VMEM((kv_count, group_rows, HD), jnp.float32),
            pltpu.VMEM((kv_count, group_rows, HD), jnp.float32),
            pltpu.VMEM((kv_count, group_rows, HD), jnp.float32),
            pltpu.VMEM((tokens, width), low),
            pltpu.VMEM((8, tokens), jnp.float32),
            pltpu.VMEM((8, tokens), jnp.float32),
            pltpu.VMEM((2, 2 * half, width), low),
            pltpu.VMEM((row_slots, width), low),
            pltpu.VMEM((2 * col_tiles, 2 * half, 2 * tile_h), low),
            pltpu.VMEM((2 * col_tiles, half, 2 * tile_h), low),
            pltpu.VMEM((2 * col_tiles, 2 * half, tile_h), low),
            pltpu.VMEM((2 * col_tiles, 2 * half, tile_f), low),
            pltpu.VMEM((2 * col_tiles, half, tile_f), low),
            pltpu.VMEM((2 * col_tiles, half, tile_f), low),
            pltpu.VMEM((col_tiles, half, tile_f), low),
            pltpu.VMEM((col_tiles, half + row_slots, tile_f), low),
            dma((3,)),
            dma((5,)),
            dma((5,)),
            dma,
            dma,
            dma((8,)),
            dma((7,)),
            dma((2 * col_tiles,)),
            dma((2 * col_tiles,)),
            dma((2 * col_tiles,)),
            dma((2 * col_tiles,)),
            dma((2 * col_tiles,)),
            dma((2 * col_tiles,)),
            dma((col_tiles,)),
            dma((col_tiles,)),
            dma((3 * col_tiles,)),
            dma((2 * col_tiles,)),
        ],
        compiler_params=pltpu.CompilerParams(
            collective_id=0, has_side_effects=True, vmem_limit_bytes=63 * 1024 * 1024
        ),
        cost_estimate=pl.CostEstimate(
            flops=10_000_000_000, bytes_accessed=40_000_000, transcendentals=3_000_000
        ),
        name="layer",
    )(
        query_rows,
        key_rows,
        value_rows,
        residual,
        segments.reshape(-1, tokens),
        routes.T,
        gate_weights.T,
        norm_gain.reshape(1, width),
        w_gate,
        w_up,
        w_down,
    )


def solution(mesh):
    in_specs = (
        P(("rep", "ep", "tc"), "tr"),
        P(("rep", "ep", "tc"), "tr"),
        P(("rep", "ep", "tc"), "tr"),
        P(("rep", "ep", "tc"), "tr"),
        P("rep"),
        P(("rep", "ep", "tc"), None),
        P(("rep", "ep", "tc"), None),
        P("tr"),
        P("tr", ("ep", "tc")),
        P("tr", ("ep", "tc")),
        P(("ep", "tc"), "tr"),
    )
    out_specs = (P(("rep", "ep", "tc"), "tr"), P(("rep", "ep", "tc"), "tr"))
    fits = (mesh.shape["ep"], mesh.shape["tr"], mesh.shape["tc"]) == (4, 2, 2)
    body = fused_shards if fits else shards
    return jax.shard_map(body, mesh=mesh, in_specs=in_specs, out_specs=out_specs, check_vma=False)
```

```python
import math

import jax
import jax.numpy as jnp
from jax import lax
from jax.experimental import pallas as pl
from jax.experimental.pallas import tpu as pltpu
from jax.sharding import PartitionSpec as P

D = 6144
QH = 48
KVH = 8
HD = 128
EXPW = 2


masked_score = -1e30
key_block = 512


def score_block(
    running, key_piece, value_piece, offset, query_heads, row_pos, row_seg, segments, score_scale
):
    best_score, denominator, accumulated = running
    length = key_piece.shape[0]
    head_count = query_heads.shape[0]
    key_heads = key_piece.reshape(length, head_count, HD)
    value_heads = value_piece.reshape(length, head_count, HD)
    key_pos = offset + jnp.arange(length, dtype=jnp.int32)
    key_seg = lax.dynamic_slice_in_dim(segments, offset, length)
    visible = (key_pos[None, :] <= row_pos[:, None]) & (key_seg[None, :] == row_seg[:, None])
    scores = (
        jnp.einsum("hrd,khd->hrk", query_heads, key_heads, preferred_element_type=jnp.float32)
        * score_scale
    )
    scores = jnp.where(visible[None], scores, masked_score)
    new_best = jnp.maximum(best_score, jnp.max(scores, axis=2))
    exponent = jnp.where(visible[None], jnp.exp(scores - new_best[:, :, None]), 0.0)
    factor = jnp.exp(best_score - new_best)
    denominator = denominator * factor + jnp.sum(exponent, axis=2)
    accumulated = accumulated * factor[:, :, None] + jnp.einsum(
        "hrk,khd->hrd",
        exponent.astype(jnp.bfloat16),
        value_heads,
        preferred_element_type=jnp.float32,
    )
    return (new_best, denominator, accumulated)


def fold_context(running, pieces, start, query_heads, row_pos, row_seg, segments, score_scale):
    key_piece, value_piece = pieces
    total_rows = key_piece.shape[0]
    for offset_rows in range(0, total_rows, key_block):
        width_rows = min(key_block, total_rows - offset_rows)
        running = score_block(
            running,
            key_piece[offset_rows : offset_rows + width_rows],
            value_piece[offset_rows : offset_rows + width_rows],
            start + offset_rows,
            query_heads,
            row_pos,
            row_seg,
            segments,
            score_scale,
        )
    return running


def shards(
    residual,
    query_rows,
    key_rows,
    value_rows,
    segments,
    routes,
    gate_weights,
    norm_gain,
    w_gate,
    w_up,
    w_down,
):
    tokens = residual.shape[0]
    feature_width = residual.shape[1]
    kv_count = key_rows.shape[1] // HD
    group_size = QH // KVH
    row_count = tokens * group_size
    first_token = lax.axis_index(("ep", "tc")) * tokens
    token_pos = first_token + jnp.arange(tokens, dtype=jnp.int32)
    token_seg = lax.dynamic_slice_in_dim(segments, first_token, tokens)
    row_pos = jnp.repeat(token_pos, group_size)
    row_seg = jnp.repeat(token_seg, group_size)
    query_heads = (
        query_rows.reshape(tokens, kv_count, group_size, HD)
        .transpose(1, 0, 2, 3)
        .reshape(kv_count, row_count, HD)
    )
    score_scale = 1.0 / math.sqrt(HD)
    initial = (
        jnp.full((kv_count, row_count), masked_score, jnp.float32),
        jnp.zeros((kv_count, row_count), jnp.float32),
        jnp.zeros((kv_count, row_count, HD), jnp.float32),
    )
    folded = fold_context(
        initial,
        (
            lax.all_gather(key_rows, ("ep", "tc"), axis=0, tiled=True),
            lax.all_gather(value_rows, ("ep", "tc"), axis=0, tiled=True),
        ),
        jnp.int32(0),
        query_heads,
        row_pos,
        row_seg,
        segments,
        score_scale,
    )
    heads_out = folded[2] / folded[1][:, :, None]
    attention = (
        heads_out.reshape(kv_count, tokens, group_size, HD)
        .transpose(1, 0, 2, 3)
        .reshape(tokens, feature_width)
        .astype(jnp.bfloat16)
    )
    mixed_rows = (residual.astype(jnp.float32) + attention.astype(jnp.float32)).astype(jnp.bfloat16)
    mixed_wide = mixed_rows.astype(jnp.float32)
    squares = lax.psum(jnp.sum(mixed_wide * mixed_wide, axis=1), "tr")
    inv_rms = lax.rsqrt(squares / D + 1e-05)
    normed = (mixed_wide * inv_rms[:, None] * norm_gain[None, :]).astype(jnp.bfloat16)
    capacity = tokens // 4
    expert_ids = jnp.arange(EXPW, dtype=jnp.int32)
    matches = routes[:, None, :] == expert_ids[None, :, None]
    chosen = jnp.any(matches, axis=2)
    weight_cols = jnp.sum(jnp.where(matches, gate_weights[:, None, :], 0.0), axis=2)
    slot_index = jnp.cumsum(chosen.astype(jnp.int32), axis=0) - 1
    slot_ids = jnp.arange(capacity, dtype=jnp.int32)
    placement_table = (slot_index.T[:, None, :] == slot_ids[None, :, None]) & chosen.T[:, None, :]
    packed = jnp.einsum(
        "ect,td->ecd",
        placement_table.astype(jnp.bfloat16),
        normed,
        preferred_element_type=jnp.float32,
    ).astype(jnp.bfloat16)
    ep_count = lax.axis_size("ep")
    tc_count = lax.axis_size("tc")
    share_count = ep_count // EXPW
    spread = jnp.repeat(packed, share_count, axis=0)
    outgoing = jnp.broadcast_to(
        spread[:, None], (ep_count, tc_count, capacity, feature_width)
    ).reshape(ep_count * tc_count, capacity, feature_width)
    arrived = lax.all_to_all(outgoing, ("ep", "tc"), split_axis=0, concat_axis=0, tiled=True)
    slot_rows = arrived.reshape(ep_count * tc_count * capacity, feature_width)
    part_gate = jnp.dot(slot_rows, w_gate, preferred_element_type=jnp.float32)
    part_up = jnp.dot(slot_rows, w_up, preferred_element_type=jnp.float32)
    gate_sum, up_sum = (
        lax.psum(part_gate.astype(jnp.bfloat16), "tr").astype(jnp.float32),
        lax.psum(part_up.astype(jnp.bfloat16), "tr").astype(jnp.float32),
    )
    hidden = (jax.nn.silu(gate_sum) * up_sum).astype(jnp.bfloat16)
    down_part = (
        jnp.dot(hidden, w_down, preferred_element_type=jnp.float32)
        .astype(jnp.bfloat16)
        .reshape(ep_count * tc_count, capacity, feature_width)
    )
    returned = lax.all_to_all(down_part, ("ep", "tc"), split_axis=0, concat_axis=0, tiled=True)
    per_expert = jnp.sum(
        returned.astype(jnp.float32).reshape(EXPW, share_count * tc_count, capacity, feature_width),
        axis=1,
    )
    combine_table = placement_table.astype(jnp.float32) * weight_cols.T[:, None, :]
    expert_mix = jnp.einsum(
        "ect,ecd->td", combine_table, per_expert, precision=lax.Precision.HIGHEST
    ).astype(jnp.bfloat16)
    return (attention, expert_mix)


col_tiles = 4
row_slots = 32
MESH = pl.DeviceIdType.MESH


def layer_kernel(
    query_ref,
    key_ref,
    value_ref,
    residual_ref,
    segment_ref,
    route_ref,
    weight_ref,
    gain_ref,
    gate_hbm,
    up_hbm,
    down_hbm,
    both_ref,
    gate_w,
    up_w,
    down_w,
    context,
    best,
    total,
    accumulated,
    mixed,
    sum_out,
    sum_in,
    slot_rows,
    cross_rows,
    parts,
    parts_in,
    hidden,
    down,
    down_in,
    reduced,
    outer_in,
    returned,
    load_sem,
    ctx_send,
    ctx_recv,
    sum_send,
    sum_recv,
    row_send,
    row_recv,
    part_send,
    part_recv,
    hid_send,
    hid_recv,
    down_send,
    down_recv,
    outer_send,
    outer_recv,
    ret_send,
    ret_recv,
):
    tokens, width = query_ref.shape
    kv_width = key_ref.shape[1]
    kv_count = kv_width // HD
    group = QH // KVH
    hidden_width = gate_w.shape[1]
    tile_h = hidden_width // col_tiles
    tile_f = width // col_tiles
    half = 2 * row_slots
    z = lax.axis_index("ep")
    x = lax.axis_index("tr")
    c = lax.axis_index("tc")
    pair = z // 2
    partner = z + 1 - 2 * lax.rem(z, 2)
    other_inner = 2 - pair
    other_outer = 3 - 3 * pair
    my_inner = 1 + pair
    my_outer = 3 * pair
    is_inner = z == my_inner
    sibling = {"tc": 1 - c}
    across = {"tr": 1 - x}

    loads = [
        pltpu.make_async_copy(gate_hbm, gate_w, load_sem.at[0]),
        pltpu.make_async_copy(up_hbm, up_w, load_sem.at[1]),
        pltpu.make_async_copy(down_hbm, down_w, load_sem.at[2]),
    ]
    for load in loads:
        load.start()

    barrier = pltpu.get_barrier_semaphore()
    for step in range(1, 4):
        there = lax.rem(z + step, 4)
        pl.semaphore_signal(barrier, inc=1, device_id={"ep": there}, device_id_type=MESH)
    pl.semaphore_signal(barrier, inc=1, device_id=sibling, device_id_type=MESH)
    pl.semaphore_signal(barrier, inc=1, device_id=across, device_id_type=MESH)

    def send(src, dst, send_sem, recv_sem, target):
        return pltpu.make_async_remote_copy(
            src_ref=src,
            dst_ref=dst,
            send_sem=send_sem,
            recv_sem=recv_sem,
            device_id=target,
            device_id_type=MESH,
        )

    own_ctx = pl.ds(pl.multiple_of(c * tokens, tokens), tokens)
    sib_ctx = pl.ds(pl.multiple_of((1 - c) * tokens, tokens), tokens)
    context[0, own_ctx, :kv_width] = key_ref[...]
    context[0, own_ctx, kv_width:] = value_ref[...]
    pl.semaphore_wait(barrier, 5)

    def ctx_copy(from_slot, to_slot, number, recv, target):
        return send(
            context.at[from_slot, own_ctx],
            context.at[to_slot, own_ctx],
            ctx_send.at[number],
            ctx_recv.at[recv],
            target,
        )

    up_chip = {"ep": lax.rem(z + 1, 4)}
    own_up = ctx_copy(0, 1, 0, 0, up_chip)
    near_up = ctx_copy(1, 2, 1, 1, up_chip)
    own_sib = ctx_copy(0, 0, 2, 2, sibling)
    near_sib = ctx_copy(1, 1, 3, 3, sibling)
    far_sib = ctx_copy(2, 2, 4, 4, sibling)

    @pl.when(z < 3)
    def _():
        own_up.start()

    own_sib.start()

    lane = lax.broadcasted_iota(jnp.int32, (tokens, tokens), 1)
    sub = lax.broadcasted_iota(jnp.int32, (tokens, tokens), 0)
    upto = jnp.where(sub <= lane, 1.0, 0.0).astype(jnp.bfloat16)

    def placement(expert):
        first = jnp.broadcast_to(route_ref[0:1, :], (tokens, tokens)) == expert
        second = jnp.broadcast_to(route_ref[1:2, :], (tokens, tokens)) == expert
        weight = jnp.where(
            first, jnp.broadcast_to(weight_ref[0:1, :], (tokens, tokens)), 0.0
        ) + jnp.where(second, jnp.broadcast_to(weight_ref[1:2, :], (tokens, tokens)), 0.0)
        named = jnp.where(first | second, 1.0, 0.0)
        order = jnp.dot(named.astype(jnp.bfloat16), upto, preferred_element_type=jnp.float32)
        wanted = (lax.rem(sub, row_slots) + 1).astype(jnp.float32)
        place = jnp.where((order == wanted) & (named > 0.5), 1.0, 0.0)
        return place, weight

    own_place, own_weight = placement(pair)
    cross_place, cross_weight = placement(1 - pair)

    scale = 1.0 / math.sqrt(HD)
    block = 2 * z + c
    row_seg = jnp.transpose(
        jnp.broadcast_to(segment_ref[pl.ds(block, 1), :].astype(jnp.float32), (tokens, tokens))
    )
    row_seg = jnp.concatenate([row_seg, row_seg], axis=1)

    def attend(slot):
        low = 2 * (z - slot)
        key_seg = jnp.concatenate(
            [segment_ref[pl.ds(low, 1), :], segment_ref[pl.ds(low + 1, 1), :]], axis=1
        ).astype(jnp.float32)
        visible = row_seg == jnp.broadcast_to(key_seg, (tokens, 2 * tokens))
        if slot == 0:
            key_pos = lax.broadcasted_iota(jnp.int32, (tokens, 2 * tokens), 1)
            row_pos = c * tokens + lax.broadcasted_iota(jnp.int32, (tokens, 2 * tokens), 0)
            visible = visible & (key_pos <= row_pos)
        bias = jnp.where(visible, 0.0, masked_score)

        def one_head(j, carry):
            heads = [
                query_ref[:, pl.ds(pl.multiple_of((j * group + g) * HD, HD), HD)]
                for g in range(group)
            ]
            queries = jnp.concatenate(heads, axis=0)
            keys = context[slot, :, pl.ds(pl.multiple_of(j * HD, HD), HD)]
            values = context[slot, :, pl.ds(pl.multiple_of(kv_width + j * HD, HD), HD)]
            scores = lax.dot_general(
                queries, keys, (((1,), (1,)), ((), ())), preferred_element_type=jnp.float32
            )
            scores = (scores * scale).reshape(group, tokens, 2 * tokens)
            scores = jnp.where((bias < -1.0)[None], masked_score, scores)
            scores = scores.reshape(group * tokens, 2 * tokens)
            peak = jnp.max(scores, axis=1, keepdims=True)
            if slot > 0:
                old = best[j][:, :1]
                peak = jnp.maximum(peak, old)
            exponent = jnp.exp(scores - peak)
            amount = jnp.sum(exponent, axis=1, keepdims=True)
            product = jnp.dot(
                exponent.astype(jnp.bfloat16), values, preferred_element_type=jnp.float32
            )
            if slot > 0:
                factor = jnp.exp(old - peak)
                amount = amount + total[j][:, :1] * factor
                product = product + accumulated[j] * factor
            best[j] = jnp.broadcast_to(peak, (group * tokens, HD))
            total[j] = jnp.broadcast_to(amount, (group * tokens, HD))
            accumulated[j] = product
            return carry

        lax.fori_loop(0, kv_count, one_head, 0)

    own_near = pl.ds(pl.multiple_of(c * half, row_slots), row_slots)
    own_far = pl.ds(pl.multiple_of(c * half + row_slots, row_slots), row_slots)

    def row_copy(chunk, place, number, recv, target):
        return send(
            slot_rows.at[chunk, place],
            slot_rows.at[chunk, place],
            row_send.at[number],
            row_recv.at[recv],
            target,
        )

    to_partner = send(
        slot_rows.at[0, own_near],
        slot_rows.at[0, own_far],
        row_send.at[0],
        row_recv.at[0],
        {"ep": partner},
    )
    cross_target = {"ep": other_inner}
    from_inner = send(
        cross_rows, slot_rows.at[1, own_near], row_send.at[1], row_recv.at[1], cross_target
    )
    from_outer = send(
        cross_rows, slot_rows.at[1, own_far], row_send.at[1], row_recv.at[2], cross_target
    )
    own_share = row_copy(0, own_near, 2, 3, sibling)
    partner_share = row_copy(0, own_far, 3, 4, sibling)
    inner_share = row_copy(1, own_near, 4, 5, sibling)
    outer_share = row_copy(1, own_far, 5, 6, sibling)
    pass_inner = row_copy(1, own_near, 6, 1, {"ep": my_outer})
    pass_outer = row_copy(1, own_far, 7, 2, {"ep": my_outer})

    def relay_cross():
        from_inner.wait_recv()

        @pl.when(is_inner)
        def _():
            pass_inner.start()

        inner_share.start()
        from_outer.wait_recv()

        @pl.when(is_inner)
        def _():
            pass_outer.start()

        outer_share.start()

    own_sib.wait_recv()
    attend(0)

    @pl.when(z >= 1)
    def _():
        own_up.wait_recv()

        @pl.when(z < 3)
        def _():
            near_up.start()

        near_sib.start()
        near_sib.wait_recv()
        attend(1)

    @pl.when(z >= 2)
    def _():
        near_up.wait_recv()
        far_sib.start()
        far_sib.wait_recv()
        attend(2)

    @pl.when(z == 2)
    def _():
        relay_cross()

    squares = jnp.zeros((tokens, HD), jnp.float32)

    def finish_head(j, squares):
        for g in range(group):
            rows = slice(g * tokens, (g + 1) * tokens)
            cols = pl.ds(pl.multiple_of((j * group + g) * HD, HD), HD)
            result = (accumulated[j, rows, :] / total[j, rows, :]).astype(jnp.bfloat16)
            both_ref[0, :, cols] = result
            both = (
                residual_ref[:, cols].astype(jnp.float32) + result.astype(jnp.float32)
            ).astype(jnp.bfloat16)
            mixed[:, cols] = both
            wide = both.astype(jnp.float32)
            squares = squares + wide * wide
        return squares

    squares = lax.fori_loop(0, kv_count, finish_head, squares)
    my_sum = jnp.broadcast_to(jnp.sum(jnp.transpose(squares), axis=0, keepdims=True), (8, tokens))
    sum_out[...] = my_sum
    sum_copy = send(sum_out, sum_in, sum_send, sum_recv, across)
    sum_copy.start()
    sum_copy.wait_recv()
    both_sums = jnp.broadcast_to((my_sum + sum_in[...])[0:1, :], (tokens, tokens))
    inv_rms = jnp.transpose(lax.rsqrt(both_sums / D + 1e-05))[:, :1]
    picks = jnp.concatenate([own_place[:row_slots], cross_place[:row_slots]], axis=0).astype(
        jnp.bfloat16
    )
    def pack(m, carry):
        cols = pl.ds(pl.multiple_of(m * tile_f, tile_f), tile_f)
        normed = (mixed[:, cols].astype(jnp.float32) * inv_rms * gain_ref[:, cols]).astype(
            jnp.bfloat16
        )
        packed = jnp.dot(picks, normed, preferred_element_type=jnp.float32).astype(jnp.bfloat16)
        slot_rows[0, own_near, cols] = packed[:row_slots]
        cross_rows[:, cols] = packed[row_slots:]
        return carry

    lax.fori_loop(0, col_tiles, pack, 0)

    @pl.when(is_inner)
    def _():
        from_inner.start()

    @pl.when(jnp.logical_not(is_inner))
    def _():
        from_outer.start()

    to_partner.start()
    own_share.start()

    def part_copy(chunk, n):
        number = chunk * col_tiles + n
        rows = pl.ds(pl.multiple_of((1 - x) * half, half), half)
        return send(
            parts.at[number, rows],
            parts_in.at[number],
            part_send.at[number],
            part_recv.at[number],
            across,
        )

    def hidden_copy(chunk, n):
        number = chunk * col_tiles + n
        rows = pl.ds(pl.multiple_of(x * half, half), half)
        return send(
            hidden.at[number, rows],
            hidden.at[number, rows],
            hid_send.at[number],
            hid_recv.at[number],
            across,
        )

    def gate_up(chunk):
        def one_tile(n, carry):
            cols = pl.ds(pl.multiple_of(n * tile_h, tile_h), tile_h)
            number = chunk * col_tiles + n
            parts[number, :, :tile_h] = jnp.dot(
                slot_rows[chunk], gate_w[:, cols], preferred_element_type=jnp.float32
            ).astype(jnp.bfloat16)
            parts[number, :, tile_h:] = jnp.dot(
                slot_rows[chunk], up_w[:, cols], preferred_element_type=jnp.float32
            ).astype(jnp.bfloat16)
            part_copy(chunk, n).start()
            return carry

        lax.fori_loop(0, col_tiles, one_tile, 0)

    def activate(chunk):
        def one_tile(n, carry):
            number = chunk * col_tiles + n
            part_copy(chunk, n).wait_recv()
            rows = pl.ds(pl.multiple_of(x * half, half), half)
            sums = parts[number, rows, :].astype(jnp.float32) + parts_in[number].astype(
                jnp.float32
            )
            gate = sums[:, :tile_h]
            hidden[number, rows, :] = (
                gate / (1.0 + jnp.exp(-gate)) * sums[:, tile_h:]
            ).astype(jnp.bfloat16)
            hidden_copy(chunk, n).start()
            return carry

        lax.fori_loop(0, col_tiles, one_tile, 0)

    def await_hidden(chunk):
        def one_tile(n, carry):
            hidden_copy(chunk, n).wait_recv()
            return carry

        lax.fori_loop(0, col_tiles, one_tile, 0)

    def down_copy(chunk, m):
        number = chunk * col_tiles + m
        rows = pl.ds(pl.multiple_of((1 - c) * half, half), half)
        return send(
            down.at[number, rows],
            down_in.at[number],
            down_send.at[number],
            down_recv.at[number],
            sibling,
        )

    def project(chunk):
        def one_tile(m, carry):
            cols = pl.ds(pl.multiple_of(m * tile_f, tile_f), tile_f)
            number = chunk * col_tiles + m
            units = jnp.concatenate(
                [hidden[chunk * col_tiles + n] for n in range(col_tiles)], axis=1
            )
            down[number] = jnp.dot(
                units, down_w[:, cols], preferred_element_type=jnp.float32
            ).astype(jnp.bfloat16)
            down_copy(chunk, m).start()
            return carry

        lax.fori_loop(0, col_tiles, one_tile, 0)

    def chip_sum(chunk, m):
        number = chunk * col_tiles + m
        down_copy(chunk, m).wait_recv()
        rows = pl.ds(pl.multiple_of(c * half, half), half)
        return down[number, rows, :].astype(jnp.float32) + down_in[number].astype(jnp.float32)

    near_rows = pl.ds(0, row_slots)
    far_rows = pl.ds(row_slots, row_slots)
    cross_back = pl.ds(half, row_slots)

    def partner_back(m):
        return send(
            reduced.at[m, far_rows],
            returned.at[m, far_rows],
            ret_send.at[m],
            ret_recv.at[m],
            {"ep": partner},
        )

    def outer_copy(m):
        return send(
            reduced.at[col_tiles + m],
            outer_in.at[m],
            outer_send.at[m],
            outer_recv.at[m],
            {"ep": my_inner},
        )

    def inner_back(m):
        return send(
            reduced.at[col_tiles + m, near_rows],
            returned.at[m, cross_back],
            ret_send.at[col_tiles + m],
            ret_recv.at[col_tiles + m],
            {"ep": other_inner},
        )

    def outer_back(m):
        return send(
            reduced.at[col_tiles + m, far_rows],
            returned.at[m, cross_back],
            ret_send.at[2 * col_tiles + m],
            ret_recv.at[col_tiles + m],
            {"ep": other_outer},
        )

    def take_own():
        to_partner.wait_recv()
        partner_share.start()
        own_share.wait_recv()
        partner_share.wait_recv()

    def take_cross():
        @pl.when(z != 2)
        def _():
            relay_cross()

        inner_share.wait_recv()
        outer_share.wait_recv()

    def take(lower_first):
        @pl.when(pair == lower_first)
        def _():
            take_own()

        @pl.when(pair != lower_first)
        def _():
            take_cross()

    def return_own():
        def one_tile(m, carry):
            sums = chip_sum(0, m).astype(jnp.bfloat16)
            returned[m, near_rows, :] = sums[:row_slots]
            reduced[m] = sums
            partner_back(m).start()
            return carry

        lax.fori_loop(0, col_tiles, one_tile, 0)

    def return_cross():
        @pl.when(jnp.logical_not(is_inner))
        def _():
            def hand_over(m, carry):
                reduced[col_tiles + m] = chip_sum(1, m).astype(jnp.bfloat16)
                outer_copy(m).start()
                return carry

            lax.fori_loop(0, col_tiles, hand_over, 0)

        @pl.when(is_inner)
        def _():
            def hand_back(m, carry):
                sums = chip_sum(1, m)
                outer_copy(m).wait_recv()
                reduced[col_tiles + m] = (sums + outer_in[m].astype(jnp.float32)).astype(
                    jnp.bfloat16
                )
                outer_back(m).start()
                inner_back(m).start()
                return carry

            lax.fori_loop(0, col_tiles, hand_back, 0)

    def give_back(lower_first):
        @pl.when(pair == lower_first)
        def _():
            return_own()

        @pl.when(pair != lower_first)
        def _():
            return_cross()

    first, second = pair, 1 - pair
    take(0)
    loads[0].wait()
    loads[1].wait()
    gate_up(first)
    activate(first)
    take(1)
    gate_up(second)
    loads[2].wait()
    await_hidden(first)
    project(first)
    give_back(0)
    activate(second)
    await_hidden(second)
    project(second)
    give_back(1)

    own_spread = jnp.transpose(own_place)[:, :half].astype(jnp.bfloat16)
    cross_spread = jnp.transpose(cross_place)[:, :row_slots].astype(jnp.bfloat16)
    own_scale = jnp.transpose(own_weight)[:, :1]
    cross_scale = jnp.transpose(cross_weight)[:, :1]

    def combine(m, carry):
        cols = pl.ds(pl.multiple_of(m * tile_f, tile_f), tile_f)
        partner_back(m).wait_recv()
        own_part = jnp.dot(own_spread, returned[m, :half, :], preferred_element_type=jnp.float32)
        inner_back(m).wait_recv()
        cross_part = jnp.dot(
            cross_spread, returned[m, half:, :], preferred_element_type=jnp.float32
        )
        both_ref[1, :, cols] = (own_scale * own_part + cross_scale * cross_part).astype(jnp.bfloat16)
        return carry

    lax.fori_loop(0, col_tiles, combine, 0)

    @pl.when(z < 3)
    def _():
        own_up.wait_send()

    @pl.when((z >= 1) & (z < 3))
    def _():
        near_up.wait_send()

    own_sib.wait_send()

    @pl.when(z >= 1)
    def _():
        near_sib.wait_send()

    @pl.when(z >= 2)
    def _():
        far_sib.wait_send()

    sum_copy.wait_send()
    for copy in (to_partner, from_inner, own_share, partner_share, inner_share, outer_share):
        copy.wait_send()

    @pl.when(is_inner)
    def _():
        pass_inner.wait_send()
        pass_outer.wait_send()

    def drain(n, carry):
        for chunk in range(2):
            part_copy(chunk, n).wait_send()
            hidden_copy(chunk, n).wait_send()
            down_copy(chunk, n).wait_send()
        partner_back(n).wait_send()
        return carry

    lax.fori_loop(0, col_tiles, drain, 0)

    @pl.when(is_inner)
    def _():
        def drain_inner(m, carry):
            inner_back(m).wait_send()
            outer_back(m).wait_send()
            return carry

        lax.fori_loop(0, col_tiles, drain_inner, 0)

    @pl.when(jnp.logical_not(is_inner))
    def _():
        def drain_outer(m, carry):
            outer_copy(m).wait_send()
            return carry

        lax.fori_loop(0, col_tiles, drain_outer, 0)


def fused_shards(
    residual,
    query_rows,
    key_rows,
    value_rows,
    segments,
    routes,
    gate_weights,
    norm_gain,
    w_gate,
    w_up,
    w_down,
):
    tokens, width = residual.shape
    kv_width = key_rows.shape[1]
    kv_count = kv_width // HD
    group_rows = tokens * (QH // KVH)
    hidden_width = w_gate.shape[1]
    tile_h = hidden_width // col_tiles
    tile_f = width // col_tiles
    half = 2 * row_slots
    low = jnp.bfloat16
    vmem = pl.BlockSpec(memory_space=pltpu.VMEM)
    hbm = pl.BlockSpec(memory_space=pl.ANY)
    dma = pltpu.SemaphoreType.DMA
    both = pl.pallas_call(
        layer_kernel,
        out_shape=jax.ShapeDtypeStruct((2, tokens, width), low),
        in_specs=[vmem] * 8 + [hbm] * 3,
        out_specs=vmem,
        scratch_shapes=[
            pltpu.VMEM(w_gate.shape, low),
            pltpu.VMEM(w_up.shape, low),
            pltpu.VMEM(w_down.shape, low),
            pltpu.VMEM((3, 2 * tokens, 2 * kv_width), low),
            pltpu.VMEM((kv_count, group_rows, HD), jnp.float32),
            pltpu.VMEM((kv_count, group_rows, HD), jnp.float32),
            pltpu.VMEM((kv_count, group_rows, HD), jnp.float32),
            pltpu.VMEM((tokens, width), low),
            pltpu.VMEM((8, tokens), jnp.float32),
            pltpu.VMEM((8, tokens), jnp.float32),
            pltpu.VMEM((2, 2 * half, width), low),
            pltpu.VMEM((row_slots, width), low),
            pltpu.VMEM((2 * col_tiles, 2 * half, 2 * tile_h), low),
            pltpu.VMEM((2 * col_tiles, half, 2 * tile_h), low),
            pltpu.VMEM((2 * col_tiles, 2 * half, tile_h), low),
            pltpu.VMEM((2 * col_tiles, 2 * half, tile_f), low),
            pltpu.VMEM((2 * col_tiles, half, tile_f), low),
            pltpu.VMEM((2 * col_tiles, half, tile_f), low),
            pltpu.VMEM((col_tiles, half, tile_f), low),
            pltpu.VMEM((col_tiles, half + row_slots, tile_f), low),
            dma((3,)),
            dma((5,)),
            dma((5,)),
            dma,
            dma,
            dma((8,)),
            dma((7,)),
            dma((2 * col_tiles,)),
            dma((2 * col_tiles,)),
            dma((2 * col_tiles,)),
            dma((2 * col_tiles,)),
            dma((2 * col_tiles,)),
            dma((2 * col_tiles,)),
            dma((col_tiles,)),
            dma((col_tiles,)),
            dma((3 * col_tiles,)),
            dma((2 * col_tiles,)),
        ],
        compiler_params=pltpu.CompilerParams(
            collective_id=0, has_side_effects=True, vmem_limit_bytes=63 * 1024 * 1024
        ),
        cost_estimate=pl.CostEstimate(
            flops=10_000_000_000, bytes_accessed=40_000_000, transcendentals=3_000_000
        ),
        name="layer",
    )(
        query_rows,
        key_rows,
        value_rows,
        residual,
        segments.reshape(-1, tokens),
        routes.T,
        gate_weights.T,
        norm_gain.reshape(1, width),
        w_gate,
        w_up,
        w_down,
    )
    return both[0], both[1]


def solution(mesh):
    in_specs = (
        P(("rep", "ep", "tc"), "tr"),
        P(("rep", "ep", "tc"), "tr"),
        P(("rep", "ep", "tc"), "tr"),
        P(("rep", "ep", "tc"), "tr"),
        P("rep"),
        P(("rep", "ep", "tc"), None),
        P(("rep", "ep", "tc"), None),
        P("tr"),
        P("tr", ("ep", "tc")),
        P("tr", ("ep", "tc")),
        P(("ep", "tc"), "tr"),
    )
    out_specs = (P(("rep", "ep", "tc"), "tr"), P(("rep", "ep", "tc"), "tr"))
    fits = (mesh.shape["ep"], mesh.shape["tr"], mesh.shape["tc"]) == (4, 2, 2)
    body = fused_shards if fits else shards
    return jax.shard_map(body, mesh=mesh, in_specs=in_specs, out_specs=out_specs, check_vma=False)
```
